32 devices in a mesh: gx: 8 (over z, x), row: 2 (over core), th: 2 (over y).
Axes of the slice: x: 2, y: 2, z: 4, core: 2. Of those that a mesh axis runs over, the one named last changes fastest.
Arguments:
- state: float32 [5, 256, 32, 256], P(None, 'gx', 'row', 'th'), may hold values from -2 to 4, as said below
- adjoint_seed: float32 [5, 256, 32, 256], P(None, 'gx', 'row', 'th'), may hold values from -6 to 6
- coef_x: float32 [9], replicated, may hold values from -1.75 to 1.75
- coef_r: float32 [9], replicated, may hold values from -1.75 to 1.75
- coef_t: float32 [9], replicated, may hold values from -1.75 to 1.75
- coef_filter: float32 [9], replicated, may hold values from -0.625 to 0.625
- metric: float32 [32], P('row'), may hold values from 0.5 to 2
Outputs:
- new_state: float32 [5, 256, 32, 256], P(None, 'gx', 'row', 'th')
- adjoint_state: float32 [5, 256, 32, 256], P(None, 'gx', 'row', 'th')
The draws below stay inside these ranges and needn't reach their ends.
Inputs may be any that keep to these rules, and one draw needn't show every extreme that they name: `state`: component 0 (density) lies in [0.5, 1.5], components 1 to 3 (momenta) in [-2, 2], component 4 (total energy) in [2, 4].
All inputs are finite; a program needn't handle non-finite values.
Results may differ from the reference program's by a relative error of at most 0.0001.
Values sent between devices are 32-bit elements; how exact they have to be, the bound alone decides.
A program may use at most 64 MiB of HBM per device.

```python
import math
import jax
import jax.numpy as jnp
from jax import lax

CX = 32
W = 4
NX = 256
NR = 32
NT = 256


def draw_state(key, part):
    keys = jax.random.split(key, 3)
    shape = (NX, NR, NT)
    density = jax.random.uniform(keys[0], shape, jnp.float32, 0.7, 1.3)
    moment = jnp.clip(0.5 * jax.random.normal(keys[1], (3,) + shape, jnp.float32), -2.0, 2.0)
    energy = jax.random.uniform(keys[2], shape, jnp.float32, 2.5, 3.5)
    return jnp.concatenate([density[None], moment, energy[None]], axis=0)


def levels(own_key, dims, shards, least, high):
    gain = 1.0
    for axis_at, parts in shards:
        draws = jax.random.uniform(jax.random.fold_in(jax.random.fold_in(own_key, 6), axis_at), (parts,), jnp.float32, least / len(shards), high / len(shards))
        gain = gain * jnp.repeat(jnp.exp(draws), dims[axis_at] // parts).reshape((-1,) + (1,) * (len(dims) - 1 - axis_at))
    return gain


def gaussian(own_key, extent, spread, bound, shards=(), kind=jnp.bfloat16):
    values = spread * jax.random.normal(own_key, extent, jnp.float32)
    if shards:
        values = values * levels(own_key, extent, shards, -0.22, 0.18)
    return jnp.clip(values, -bound, bound).astype(kind)


def setup_inputs(seed: int = 0) -> dict:
    streams_of = jax.random.split(jax.random.key(seed), 8)
    return {
        "state": draw_state(jax.random.fold_in(streams_of[7], 71), 0),
        "adjoint_seed": gaussian(streams_of[1], (5, NX, NR, NT), 1.0, 6.0, ((1, 8), (2, 2), (3, 2)), jnp.float32),
        "coef_x": gaussian(streams_of[2], (2 * W + 1,), 0.3, 1.75, (), jnp.float32),
        "coef_r": gaussian(streams_of[3], (2 * W + 1,), 0.3, 1.75, (), jnp.float32),
        "coef_t": gaussian(streams_of[4], (2 * W + 1,), 0.3, 1.75, (), jnp.float32),
        "coef_filter": gaussian(streams_of[5], (2 * W + 1,), 0.1, 0.625, (), jnp.float32),
        "metric": jnp.clip(jnp.exp(math.log(2.0) - 1.3862944 * jax.random.uniform(streams_of[6], (NR,), jnp.float32) ** levels(streams_of[6], (NR,), ((0, 2),), -0.2, 0.2)), 0.5, 2.0),
    }


section_dt = 0.1
gamma_less = 0.4

def fluxes(state):
    density = state[0]
    velocity = state[1:4] / density
    pressure = gamma_less * (state[4] - 0.5 * lax.optimization_barrier(jnp.sum(state[1:4] * velocity, axis=0)))
    enthalpy = state[4] + pressure
    result = []
    for direction in range(3):
        speed = velocity[direction]
        moment = state[1:4] * speed
        moment = moment.at[direction].add(pressure)
        result.append(jnp.concatenate([state[1 + direction][None], moment, (enthalpy * speed)[None]], axis=0))
    return result

def stencil_sum(field, coef, axis, periodic):
    reach = (coef.shape[0] - 1) // 2
    widths = [(0, 0)] * field.ndim
    widths[axis] = (reach, reach)
    if periodic:
        padded = jnp.pad(field, widths, mode='wrap')
    else:
        padded = jnp.pad(field, widths)
    count = field.shape[axis]
    total = jnp.zeros(field.shape, field.dtype)
    for tap in range(coef.shape[0]):
        total = total + coef[tap] * lax.slice_in_dim(padded, tap, tap + count, axis=axis)
    return total

def slab_sum(field, coef, low, count):
    reach = (coef.shape[0] - 1) // 2
    shape = (field.shape[0], count, field.shape[2], field.shape[3])
    total = jnp.zeros(shape, field.dtype)
    for tap in range(coef.shape[0]):
        begin = low + tap - reach
        total = total + coef[tap] * lax.slice_in_dim(field, begin, begin + count, axis=1)
    return total

def reference(state, adjoint_seed, coef_x, coef_r, coef_t, coef_filter, metric):
    margin = 2 * W
    width = CX + 4 * W
    total_x = state.shape[1]
    filler = jnp.array([1.0, 0.0, 0.0, 0.0, 3.0], dtype=state.dtype)[:, None, None, None]
    padded_state = jnp.pad(state - filler, ((0, 0), (margin, margin), (0, 0), (0, 0))) + filler
    padded_adjoint = jnp.pad(adjoint_seed, ((0, 0), (margin, margin), (0, 0), (0, 0)))
    weight_r = metric[None, None, :, None]
    flip_filter = coef_filter[::-1]
    flip_x = coef_x[::-1]
    flip_r = coef_r[::-1]
    flip_t = coef_t[::-1]

    def block(index, outs):
        new_out, adj_out = outs
        start = (index * CX).astype(jnp.int32)
        slab = lax.dynamic_slice_in_dim(padded_state, start, width, axis=1)
        seed_slab = lax.dynamic_slice_in_dim(padded_adjoint, start, width, axis=1)
        position = start - margin + jnp.arange(width, dtype=jnp.int32)
        inside = ((position >= 0) & (position < total_x))[None, :, None, None]
        flux_x, flux_r, flux_t = fluxes(slab)
        flux_x = jnp.where(inside, flux_x, 0.0)
        span = CX + 2 * W
        mid_inside = inside[:, W:W + span]
        resid = -(slab_sum(flux_x, coef_x, W, span) + stencil_sum(flux_r[:, W:W + span], coef_r, 2, False) + weight_r * stencil_sum(flux_t[:, W:W + span], coef_t, 3, True))
        section = slab[:, W:W + span] + section_dt * resid
        section = jnp.where(mid_inside, section, 0.0)
        new_block = section[:, W:W + CX] - slab_sum(section, coef_filter, W, CX)
        lam_section = seed_slab[:, W:W + span] - slab_sum(seed_slab, flip_filter, W, span)
        lam_section = jnp.where(mid_inside, lam_section, 0.0)
        lam_resid = section_dt * lam_section
        grad_x = -slab_sum(lam_resid, flip_x, W, CX)
        lam_inner = lam_resid[:, W:W + CX]
        grad_r = -stencil_sum(lam_inner, flip_r, 2, False)
        grad_t = -stencil_sum(weight_r * lam_inner, flip_t, 3, True)
        _, pull = jax.vjp(fluxes, slab[:, margin:margin + CX])
        flux_grad, = pull([grad_x, grad_r, grad_t])
        adj_block = lam_section[:, W:W + CX] + flux_grad
        zero = jnp.zeros((), jnp.int32)
        new_out = lax.dynamic_update_slice(new_out, new_block, (zero, start, zero, zero))
        adj_out = lax.dynamic_update_slice(adj_out, adj_block, (zero, start, zero, zero))
        return (new_out, adj_out)
    empty = jnp.zeros(state.shape, state.dtype)
    new_state, adjoint_state = lax.fori_loop(0, total_x // CX, block, (empty, empty))
    return (new_state, adjoint_state)
```

```python
import functools

import jax
import jax.numpy as jnp
from jax import lax
from jax.experimental import pallas as pl
from jax.experimental.pallas import tpu as pltpu
from jax.sharding import PartitionSpec as P

section_dt = 0.1
gamma_less = 0.4
highest = lax.Precision.HIGHEST
MESH = pl.DeviceIdType.MESH
PAD = 8


def velocities(q):
    inv = 1.0 / q[0]
    vel = [q[1 + k] * inv for k in range(3)]
    kinetic = q[1] * vel[0] + q[2] * vel[1] + q[3] * vel[2]
    pressure = gamma_less * (q[4] - 0.5 * kinetic)
    return inv, vel, pressure, q[4] + pressure


def pull_back(q, grads):
    inv, vel, _, enthalpy = velocities(q)
    mom = q[1:4]
    a_enth = sum(grads[d][4] * vel[d] for d in range(3))
    a_pres = grads[0][1] + grads[1][2] + grads[2][3] + a_enth
    half = 0.5 * gamma_less * a_pres
    a_vel = [
        mom[0] * grads[d][1] + mom[1] * grads[d][2] + mom[2] * grads[d][3]
        + enthalpy * grads[d][4] - half * mom[d]
        for d in range(3)
    ]
    scaled = [a * inv for a in a_vel]
    a_mom = [
        grads[0][1 + k] * vel[0] + grads[1][1 + k] * vel[1] + grads[2][1 + k] * vel[2]
        + grads[k][0] - half * vel[k] + scaled[k]
        for k in range(3)
    ]
    a_dens = -(scaled[0] * vel[0] + scaled[1] * vel[1] + scaled[2] * vel[2])
    return [a_dens] + a_mom + [a_enth + gamma_less * a_pres]


def kernel(
    counts, state, seed, coef_x, coef_r, coef_t, coef_f, metric, new_out, adj_out,
    ST, SEED, FX, FR, FT, LAM, SEC, SSEND, TT, NEW, ADJ, BAND, MET, RIM, HALO,
    local_sem, send_sem, recv_sem,
):
    comps, X, R, T = state.shape
    taps = coef_x.shape[0]
    W = (taps - 1) // 2
    rim = 2 * W
    G = T // rim
    nx, nr = counts
    gx, row, th = lax.axis_index("gx"), lax.axis_index("row"), lax.axis_index("th")
    has_l, has_r = gx > 0, gx < nx - 1
    has_d, has_u = row > 0, row < nr - 1
    left, right = {"gx": lax.rem(gx + nx - 1, nx)}, {"gx": lax.rem(gx + 1, nx)}
    down, up = {"row": lax.rem(row + nr - 1, nr)}, {"row": lax.rem(row + 1, nr)}
    partner = {"th": 1 - th}

    load_state = pltpu.make_async_copy(state, ST, local_sem.at[0])
    load_seed = pltpu.make_async_copy(seed, SEED.at[:, pl.ds(2 * W, X)], local_sem.at[1])
    load_state.start()
    load_seed.start()

    barrier = pltpu.get_barrier_semaphore()
    for cond, device in ((has_l, left), (has_r, right), (has_d, down), (has_u, up)):
        @pl.when(cond)
        def _(device=device):
            pl.semaphore_signal(barrier, inc=1, device_id=device, device_id_type=MESH)
    pl.semaphore_signal(barrier, inc=1, device_id=partner, device_id_type=MESH)

    cx = [coef_x[j] for j in range(taps)]
    cr = [coef_r[j] for j in range(taps)]
    ct = [coef_t[j] for j in range(taps)]
    cf = [coef_f[j] for j in range(taps)]
    dx = [-section_dt * c for c in cx]
    dr = [-section_dt * c for c in cr]

    def remote(src, dst, k, device):
        return pltpu.make_async_remote_copy(
            src_ref=src, dst_ref=dst, send_sem=send_sem.at[k], recv_sem=recv_sem.at[k],
            device_id=device, device_id_type=MESH,
        )

    seed_up = remote(seed.at[:, pl.ds(X - 2 * W, 2 * W)], SEED.at[:, pl.ds(0, 2 * W)], 0, right)
    seed_dn = remote(seed.at[:, pl.ds(0, 2 * W)], SEED.at[:, pl.ds(X + 2 * W, 2 * W)], 1, left)
    fx_up = remote(FX.at[:, pl.ds(X, W)], FX.at[:, pl.ds(0, W)], 2, right)
    fx_dn = remote(FX.at[:, pl.ds(W, W)], FX.at[:, pl.ds(X + W, W)], 3, left)
    sec_up = remote(SSEND.at[1], SEC.at[:, pl.ds(0, W)], 4, right)
    sec_dn = remote(SSEND.at[0], SEC.at[:, pl.ds(X + W, W)], 5, left)
    fr_up = remote(FR.at[:, :, pl.ds(R, PAD)], FR.at[:, :, pl.ds(0, PAD)], 6, up)
    fr_dn = remote(FR.at[:, :, pl.ds(PAD, PAD)], FR.at[:, :, pl.ds(PAD + R, PAD)], 7, down)
    own_x = pl.ds(W, X)
    lam_up = remote(LAM.at[:, own_x, pl.ds(R, PAD)], LAM.at[:, own_x, pl.ds(0, PAD)], 8, up)
    lam_dn = remote(
        LAM.at[:, own_x, pl.ds(PAD, PAD)], LAM.at[:, own_x, pl.ds(PAD + R, PAD)], 9, down
    )
    ft_rim = remote(RIM.at[0], HALO.at[0], 10, partner)
    lam_rim = remote(RIM.at[1], HALO.at[1], 11, partner)

    def both(up_copy, dn_copy, lower, upper, what):
        if what == "start":
            pl.when(upper)(up_copy.start)
            pl.when(lower)(dn_copy.start)
        elif what == "recv":
            pl.when(lower)(up_copy.wait_recv)
            pl.when(upper)(dn_copy.wait_recv)
        else:
            pl.when(upper)(up_copy.wait_send)
            pl.when(lower)(dn_copy.wait_send)

    arrivals = sum(c.astype(jnp.int32) for c in (has_l, has_r, has_d, has_u)) + 1
    pl.semaphore_wait(barrier, arrivals)
    both(seed_up, seed_dn, has_l, has_r, "start")

    load_state.wait()

    def flux_step(x, _):
        q = [ST[v, x] for v in range(comps)]
        _, vel, pressure, enthalpy = velocities(q)
        for d in range(3):
            f = [q[1 + d]] + [q[1 + k] * vel[d] for k in range(3)] + [enthalpy * vel[d]]
            f[1 + d] = f[1 + d] + pressure
            for v in range(comps):
                if d == 0:
                    FX[v, x + W] = f[v]
                elif d == 1:
                    FR[v, x, pl.ds(PAD, R)] = f[v]
                else:
                    FT[v, x] = f[v]
        return 0

    lax.fori_loop(0, X, flux_step, 0)
    both(fr_up, fr_dn, has_d, has_u, "start")

    lane = lax.broadcasted_iota(jnp.int32, (R, T), 1) // rim

    def pack(slot, read):
        def step(v, _):
            for g in range(X // G):
                acc = jnp.zeros((R, T), jnp.float32)
                for k in range(G):
                    rolled = pltpu.roll(read(v, g * G + k), (rim * k + W) % T, 1)
                    acc = jnp.where(lane == k, rolled, acc)
                RIM[slot, v, g] = acc
            return 0
        lax.fori_loop(0, comps, step, 0)

    pack(0, lambda v, x: FT[v, x])
    ft_rim.start()
    both(fx_up, fx_dn, has_l, has_r, "start")

    def clear(cond, ref, index):
        @pl.when(cond)
        def _():
            def step(v, _):
                target = ref.at[v].at[index]
                target[...] = jnp.zeros(target.shape, jnp.float32)
                return 0
            lax.fori_loop(0, comps, step, 0)

    no_l, no_r, no_d, no_u = gx == 0, gx == nx - 1, row == 0, row == nr - 1
    everything = pl.ds(0, R)
    clear(no_l, SEED, (pl.ds(0, 2 * W),))
    clear(no_r, SEED, (pl.ds(X + 2 * W, 2 * W),))
    clear(no_l, FX, (pl.ds(0, W),))
    clear(no_r, FX, (pl.ds(X + W, W),))
    clear(no_l, SEC, (pl.ds(0, W),))
    clear(no_r, SEC, (pl.ds(X + W, W),))
    clear(no_d, FR, (pl.ds(0, X), pl.ds(0, PAD)))
    clear(no_u, FR, (pl.ds(0, X), pl.ds(PAD + R, PAD)))
    clear(no_d, LAM, (own_x, pl.ds(0, PAD)))
    clear(no_u, LAM, (own_x, pl.ds(PAD + R, PAD)))

    k_at = lax.broadcasted_iota(jnp.int32, (2 * T, T), 0)
    n_at = lax.broadcasted_iota(jnp.int32, (2 * T, T), 1)
    position = jnp.where(k_at < T, k_at, jnp.where(k_at < T + W, k_at - T - W, k_at - W))
    offset = jnp.where(k_at < T + rim, position - n_at, 2 * T)
    for slot in range(2):
        band = jnp.zeros((2 * T, T), jnp.float32)
        for j in range(taps):
            hit = offset == ((j - W) if slot == 0 else (W - j))
            band = jnp.where(hit, ct[j], band)
        BAND[slot] = band
    row_at = lax.broadcasted_iota(jnp.int32, (R, T), 0)
    weight = jnp.zeros((R, T), jnp.float32)
    for i in range(R):
        weight = jnp.where(row_at == i, metric[i], weight)
    MET[...] = -section_dt * weight

    def azimuthal(slot, read):
        def step(v, _):
            for g in range(X // G):
                own = read(v, g * G).reshape(G * R, T)
                halo = HALO[slot, v, g]
                rims = jnp.concatenate(
                    [halo if k == 0 else pltpu.roll(halo, T - rim * k, 1) for k in range(G)], axis=0
                )
                out = jnp.dot(
                    jnp.concatenate([own, rims], axis=1), BAND[slot],
                    precision=highest, preferred_element_type=jnp.float32,
                )
                TT[v, pl.ds(g * G, G)] = out.reshape(G, R, T) * MET[...][None]
            return 0
        lax.fori_loop(0, comps, step, 0)

    def lam_block(v, at, count):
        block = SEED[v, pl.ds(at, count + 2 * W)]
        total = block[W : W + count]
        for j in range(taps):
            total = total - cf[taps - 1 - j] * block[j : j + count]
        LAM[v, pl.ds(at, count), pl.ds(PAD, R)] = total

    load_seed.wait()

    def lam_inner(v, _):
        def step(c, _):
            lam_block(v, 2 * W + c * W, W)
            return 0
        return lax.fori_loop(0, (X - 2 * W) // W, step, 0)

    lax.fori_loop(0, comps, lam_inner, 0)

    both(fr_up, fr_dn, has_d, has_u, "recv")
    ft_rim.wait_recv()
    azimuthal(0, lambda v, x: FT[v, pl.ds(x, G)])

    def section_at(v, x, lo, hi):
        total = ST[v, x] + TT[v, x]
        for j in range(taps):
            total = total + dr[j] * FR[v, x, pl.ds(PAD - W + j, R)]
        for j in range(lo, hi):
            total = total + dx[j] * FX[v, x + j]
        return total

    def section_edge(v, _):
        for o in range(W):
            low = section_at(v, o, W - o, taps)
            SSEND[0, v, o] = low
            SEC[v, W + o] = low
            x = X - W + o
            high = section_at(v, x, 0, taps - 1 - o)
            SSEND[1, v, o] = high
            SEC[v, W + x] = high
        return 0

    lax.fori_loop(0, comps, section_edge, 0)
    both(sec_up, sec_dn, has_l, has_r, "start")

    def section_inner(v, _):
        def step(c, _):
            for o in range(2):
                x = W + 2 * c + o
                SEC[v, W + x] = section_at(v, x, 0, taps)
            return 0
        return lax.fori_loop(0, (X - 2 * W) // 2, step, 0)

    lax.fori_loop(0, comps, section_inner, 0)

    both(seed_up, seed_dn, has_l, has_r, "recv")

    def lam_edges(v, _):
        for at in (0, W, X, X + W):
            lam_block(v, at, W)
        return 0

    lax.fori_loop(0, comps, lam_edges, 0)
    clear(no_l, LAM, (pl.ds(0, W), pl.ds(PAD, R)))
    clear(no_r, LAM, (pl.ds(X + W, W), pl.ds(PAD, R)))
    both(lam_up, lam_dn, has_d, has_u, "start")
    pack(1, lambda v, x: LAM[v, x + W, pl.ds(PAD, R)])
    lam_rim.start()

    both(fx_up, fx_dn, has_l, has_r, "recv")

    def section_rest(v, _):
        for o in range(W):
            low = SEC[v, W + o]
            for j in range(W - o):
                low = low + dx[j] * FX[v, o + j]
            SEC[v, W + o] = low
            x = X - W + o
            high = SEC[v, W + x]
            for j in range(taps - 1 - o, taps):
                high = high + dx[j] * FX[v, x + j]
            SEC[v, W + x] = high
        return 0

    lax.fori_loop(0, comps, section_rest, 0)

    def new_block(v, x, count):
        block = SEC[v, pl.ds(x, count + 2 * W)]
        total = block[W : W + count]
        for j in range(taps):
            total = total - cf[j] * block[j : j + count]
        NEW[v, pl.ds(x, count)] = total

    def new_inner(v, _):
        def step(c, _):
            new_block(v, W + c * W, W)
            return 0
        return lax.fori_loop(0, (X - 2 * W) // W, step, 0)

    lax.fori_loop(0, comps, new_inner, 0)
    inner = pl.ds(W, X - 2 * W)
    store_inner = pltpu.make_async_copy(NEW.at[:, inner], new_out.at[:, inner], local_sem.at[2])
    store_inner.start()

    both(lam_up, lam_dn, has_d, has_u, "recv")
    lam_rim.wait_recv()
    azimuthal(1, lambda v, x: LAM[v, pl.ds(x + W, G), pl.ds(PAD, R)])

    def adjoint_step(x, _):
        q = [ST[v, x] for v in range(comps)]
        grads = [[], [], []]
        for v in range(comps):
            along_x = dx[taps - 1] * LAM[v, x, pl.ds(PAD, R)]
            along_r = dr[taps - 1] * LAM[v, x + W, pl.ds(PAD - W, R)]
            for j in range(1, taps):
                along_x = along_x + dx[taps - 1 - j] * LAM[v, x + j, pl.ds(PAD, R)]
                along_r = along_r + dr[taps - 1 - j] * LAM[v, x + W, pl.ds(PAD - W + j, R)]
            grads[0].append(along_x)
            grads[1].append(along_r)
            grads[2].append(TT[v, x])
        result = pull_back(q, grads)
        for v in range(comps):
            ADJ[v, x] = LAM[v, x + W, pl.ds(PAD, R)] + result[v]
        return 0

    lax.fori_loop(0, X, adjoint_step, 0)
    store_adj = pltpu.make_async_copy(ADJ, adj_out, local_sem.at[3])
    store_adj.start()

    both(sec_up, sec_dn, has_l, has_r, "recv")

    @pl.when(has_l)
    def _():
        def step(v, _):
            for o in range(W):
                total = SEC[v, o]
                for j in range(taps - 1 - o, taps):
                    total = total + dx[j] * FX[v, o + j - W]
                SEC[v, o] = total
            return 0
        lax.fori_loop(0, comps, step, 0)

    @pl.when(has_r)
    def _():
        def step(v, _):
            for o in range(W):
                total = SEC[v, X + W + o]
                for j in range(W - o):
                    total = total + dx[j] * FX[v, X + o + j]
                SEC[v, X + W + o] = total
            return 0
        lax.fori_loop(0, comps, step, 0)

    def new_edges(v, _):
        new_block(v, 0, W)
        new_block(v, X - W, W)
        return 0

    lax.fori_loop(0, comps, new_edges, 0)
    low, high = pl.ds(0, W), pl.ds(X - W, W)
    store_low = pltpu.make_async_copy(NEW.at[:, low], new_out.at[:, low], local_sem.at[4])
    store_high = pltpu.make_async_copy(NEW.at[:, high], new_out.at[:, high], local_sem.at[5])
    store_low.start()
    store_high.start()

    both(seed_up, seed_dn, has_l, has_r, "send")
    both(fx_up, fx_dn, has_l, has_r, "send")
    both(sec_up, sec_dn, has_l, has_r, "send")
    both(fr_up, fr_dn, has_d, has_u, "send")
    both(lam_up, lam_dn, has_d, has_u, "send")
    ft_rim.wait_send()
    lam_rim.wait_send()
    store_inner.wait()
    store_adj.wait()
    store_low.wait()
    store_high.wait()


def shards(state, adjoint_seed, coef_x, coef_r, coef_t, coef_filter, metric):
    comps, X, R, T = state.shape
    W = (coef_x.shape[0] - 1) // 2
    G = T // (2 * W)
    counts = (lax.axis_size("gx"), lax.axis_size("row"))
    anywhere = pl.BlockSpec(memory_space=pl.ANY)
    scalars = pl.BlockSpec(memory_space=pltpu.SMEM)
    f32 = jnp.float32
    shape = jax.ShapeDtypeStruct(state.shape, f32)
    return pl.pallas_call(
        functools.partial(kernel, counts),
        out_shape=(shape, shape),
        in_specs=[anywhere, anywhere] + [scalars] * 5,
        out_specs=(anywhere, anywhere),
        scratch_shapes=[
            pltpu.VMEM((comps, X, R, T), f32),
            pltpu.VMEM((comps, X + 4 * W, R, T), f32),
            pltpu.VMEM((comps, X + 2 * W, R, T), f32),
            pltpu.VMEM((comps, X, R + 2 * PAD, T), f32),
            pltpu.VMEM((comps, X, R, T), f32),
            pltpu.VMEM((comps, X + 2 * W, R + 2 * PAD, T), f32),
            pltpu.VMEM((comps, X + 2 * W, R, T), f32),
            pltpu.VMEM((2, comps, W, R, T), f32),
            pltpu.VMEM((comps, X, R, T), f32),
            pltpu.VMEM((comps, X, R, T), f32),
            pltpu.VMEM((comps, X, R, T), f32),
            pltpu.VMEM((2, 2 * T, T), f32),
            pltpu.VMEM((R, T), f32),
            pltpu.VMEM((2, comps, X // G, R, T), f32),
            pltpu.VMEM((2, comps, X // G, R, T), f32),
            pltpu.SemaphoreType.DMA((6,)),
            pltpu.SemaphoreType.DMA((12,)),
            pltpu.SemaphoreType.DMA((12,)),
        ],
        compiler_params=pltpu.CompilerParams(
            collective_id=0, has_side_effects=True, vmem_limit_bytes=40 * 2**20
        ),
    )(state, adjoint_seed, coef_x, coef_r, coef_t, coef_filter, metric)


def solution(mesh):
    placed = (P(None, "gx", "row", "th"), P(None, "gx", "row", "th"), P(), P(), P(), P(), P("row"))
    return jax.shard_map(
        shards,
        mesh=mesh,
        in_specs=placed,
        out_specs=(P(None, "gx", "row", "th"), P(None, "gx", "row", "th")),
        check_vma=False,
    )
```

```python
import functools

import jax
import jax.numpy as jnp
from jax import lax
from jax.experimental import pallas as pl
from jax.experimental.pallas import tpu as pltpu
from jax.sharding import PartitionSpec as P

section_dt = 0.1
gamma_less = 0.4
MESH = pl.DeviceIdType.MESH
PAD = 8


def velocities(q):
    inv = 1.0 / q[0]
    vel = [q[1 + k] * inv for k in range(3)]
    kinetic = q[1] * vel[0] + q[2] * vel[1] + q[3] * vel[2]
    pressure = gamma_less * (q[4] - 0.5 * kinetic)
    return inv, vel, pressure, q[4] + pressure


def pull_back(q, grads):
    inv, vel, _, enthalpy = velocities(q)
    mom = q[1:4]
    a_enth = sum(grads[d][4] * vel[d] for d in range(3))
    a_pres = grads[0][1] + grads[1][2] + grads[2][3] + a_enth
    half = 0.5 * gamma_less * a_pres
    a_vel = [
        mom[0] * grads[d][1] + mom[1] * grads[d][2] + mom[2] * grads[d][3]
        + enthalpy * grads[d][4] - half * mom[d]
        for d in range(3)
    ]
    scaled = [a * inv for a in a_vel]
    a_mom = [
        grads[0][1 + k] * vel[0] + grads[1][1 + k] * vel[1] + grads[2][1 + k] * vel[2]
        + grads[k][0] - half * vel[k] + scaled[k]
        for k in range(3)
    ]
    a_dens = -(scaled[0] * vel[0] + scaled[1] * vel[1] + scaled[2] * vel[2])
    return [a_dens] + a_mom + [a_enth + gamma_less * a_pres]


def kernel(
    counts, state, seed, coef_x, coef_r, coef_t, coef_f, metric, new_out, adj_out,
    ST, SEED, FX, FR, FT, LAM, SEC, SSEND, TT, NEW, ADJ, BAND, MET, RIM, HALO,
    local_sem, send_sem, recv_sem,
):
    comps, X, R, T = state.shape
    taps = coef_x.shape[0]
    W = (taps - 1) // 2
    rim = 2 * W
    G = T // rim
    nx, nr = counts
    gx, row, th = lax.axis_index("gx"), lax.axis_index("row"), lax.axis_index("th")
    has_l, has_r = gx > 0, gx < nx - 1
    has_d, has_u = row > 0, row < nr - 1
    left, right = {"gx": lax.rem(gx + nx - 1, nx)}, {"gx": lax.rem(gx + 1, nx)}
    down, up = {"row": lax.rem(row + nr - 1, nr)}, {"row": lax.rem(row + 1, nr)}
    partner = {"th": 1 - th}

    load_state = pltpu.make_async_copy(state, ST, local_sem.at[0])
    load_seed = pltpu.make_async_copy(seed, SEED.at[:, pl.ds(2 * W, X)], local_sem.at[1])
    load_state.start()
    load_seed.start()

    barrier = pltpu.get_barrier_semaphore()
    for cond, device in ((has_l, left), (has_r, right), (has_d, down), (has_u, up)):
        @pl.when(cond)
        def _(device=device):
            pl.semaphore_signal(barrier, inc=1, device_id=device, device_id_type=MESH)
    pl.semaphore_signal(barrier, inc=1, device_id=partner, device_id_type=MESH)

    cx = [coef_x[j] for j in range(taps)]
    cr = [coef_r[j] for j in range(taps)]
    ct = [coef_t[j] for j in range(taps)]
    cf = [coef_f[j] for j in range(taps)]
    dx = [-section_dt * c for c in cx]
    dr = [-section_dt * c for c in cr]

    def remote(src, dst, k, device):
        return pltpu.make_async_remote_copy(
            src_ref=src, dst_ref=dst, send_sem=send_sem.at[k], recv_sem=recv_sem.at[k],
            device_id=device, device_id_type=MESH,
        )

    seed_up = remote(seed.at[:, pl.ds(X - 2 * W, 2 * W)], SEED.at[:, pl.ds(0, 2 * W)], 0, right)
    seed_dn = remote(seed.at[:, pl.ds(0, 2 * W)], SEED.at[:, pl.ds(X + 2 * W, 2 * W)], 1, left)
    fx_up = remote(FX.at[:, pl.ds(X, W)], FX.at[:, pl.ds(0, W)], 2, right)
    fx_dn = remote(FX.at[:, pl.ds(W, W)], FX.at[:, pl.ds(X + W, W)], 3, left)
    sec_up = remote(SSEND.at[1], SEC.at[:, pl.ds(0, W)], 4, right)
    sec_dn = remote(SSEND.at[0], SEC.at[:, pl.ds(X + W, W)], 5, left)
    fr_up = remote(FR.at[:, :, pl.ds(R, PAD)], FR.at[:, :, pl.ds(0, PAD)], 6, up)
    fr_dn = remote(FR.at[:, :, pl.ds(PAD, PAD)], FR.at[:, :, pl.ds(PAD + R, PAD)], 7, down)
    own_x = pl.ds(W, X)
    lam_up = remote(LAM.at[:, own_x, pl.ds(R, PAD)], LAM.at[:, own_x, pl.ds(0, PAD)], 8, up)
    lam_dn = remote(
        LAM.at[:, own_x, pl.ds(PAD, PAD)], LAM.at[:, own_x, pl.ds(PAD + R, PAD)], 9, down
    )
    ft_rim = remote(RIM.at[0], HALO.at[0], 10, partner)
    lam_rim = remote(RIM.at[1], HALO.at[1], 11, partner)

    def both(up_copy, dn_copy, lower, upper, what):
        if what == "start":
            pl.when(upper)(up_copy.start)
            pl.when(lower)(dn_copy.start)
        elif what == "recv":
            pl.when(lower)(up_copy.wait_recv)
            pl.when(upper)(dn_copy.wait_recv)
        else:
            pl.when(upper)(up_copy.wait_send)
            pl.when(lower)(dn_copy.wait_send)

    arrivals = sum(c.astype(jnp.int32) for c in (has_l, has_r, has_d, has_u)) + 1
    pl.semaphore_wait(barrier, arrivals)
    both(seed_up, seed_dn, has_l, has_r, "start")

    load_state.wait()

    def flux_step(x, _):
        q = [ST[v, x] for v in range(comps)]
        _, vel, pressure, enthalpy = velocities(q)
        for d in range(3):
            f = [q[1 + d]] + [q[1 + k] * vel[d] for k in range(3)] + [enthalpy * vel[d]]
            f[1 + d] = f[1 + d] + pressure
            for v in range(comps):
                if d == 0:
                    FX[v, x + W] = f[v]
                elif d == 1:
                    FR[v, x, pl.ds(PAD, R)] = f[v]
                else:
                    FT[v, x] = f[v]
        return 0

    lax.fori_loop(0, X, flux_step, 0)
    both(fx_up, fx_dn, has_l, has_r, "start")
    both(fr_up, fr_dn, has_d, has_u, "start")

    lane = lax.broadcasted_iota(jnp.int32, (R, T), 1) // rim

    def pack(slot, read):
        def step(v, _):
            for g in range(X // G):
                acc = jnp.zeros((R, T), jnp.float32)
                for k in range(G):
                    rolled = pltpu.roll(read(v, g * G + k), (rim * k + W) % T, 1)
                    acc = jnp.where(lane == k, rolled, acc)
                RIM[slot, v, g] = acc
            return 0
        lax.fori_loop(0, comps, step, 0)

    pack(0, lambda v, x: FT[v, x])
    ft_rim.start()

    def clear(cond, ref, index):
        @pl.when(cond)
        def _():
            def step(v, _):
                target = ref.at[v].at[index]
                target[...] = jnp.zeros(target.shape, jnp.float32)
                return 0
            lax.fori_loop(0, comps, step, 0)

    no_l, no_r, no_d, no_u = gx == 0, gx == nx - 1, row == 0, row == nr - 1
    everything = pl.ds(0, R)
    clear(no_l, SEED, (pl.ds(0, 2 * W),))
    clear(no_r, SEED, (pl.ds(X + 2 * W, 2 * W),))
    clear(no_l, FX, (pl.ds(0, W),))
    clear(no_r, FX, (pl.ds(X + W, W),))
    clear(no_l, SEC, (pl.ds(0, W),))
    clear(no_r, SEC, (pl.ds(X + W, W),))
    clear(no_d, FR, (pl.ds(0, X), pl.ds(0, PAD)))
    clear(no_u, FR, (pl.ds(0, X), pl.ds(PAD + R, PAD)))
    clear(no_d, LAM, (own_x, pl.ds(0, PAD)))
    clear(no_u, LAM, (own_x, pl.ds(PAD + R, PAD)))

    k_at = lax.broadcasted_iota(jnp.int32, (2 * T, T), 0)
    n_at = lax.broadcasted_iota(jnp.int32, (2 * T, T), 1)
    position = jnp.where(k_at < T, k_at, jnp.where(k_at < T + W, k_at - T - W, k_at - W))
    offset = jnp.where(k_at < T + rim, position - n_at, 2 * T)
    for slot in range(2):
        band = jnp.zeros((2 * T, T), jnp.float32)
        for j in range(taps):
            hit = offset == ((j - W) if slot == 0 else (W - j))
            band = jnp.where(hit, ct[j], band)
        upper = band.astype(jnp.bfloat16)
        BAND[slot, 0] = upper
        BAND[slot, 1] = (band - upper.astype(jnp.float32)).astype(jnp.bfloat16)
    row_at = lax.broadcasted_iota(jnp.int32, (R, T), 0)
    weight = jnp.zeros((R, T), jnp.float32)
    for i in range(R):
        weight = jnp.where(row_at == i, metric[i], weight)
    MET[...] = -section_dt * weight

    def azimuthal(slot, read):
        def step(v, _):
            for g in range(X // G):
                own = read(v, g * G).reshape(G * R, T)
                halo = HALO[slot, v, g]
                rims = jnp.concatenate(
                    [halo if k == 0 else pltpu.roll(halo, T - rim * k, 1) for k in range(G)], axis=0
                )
                both_parts = jnp.concatenate([own, rims], axis=1)
                upper = both_parts.astype(jnp.bfloat16)
                lower = (both_parts - upper.astype(jnp.float32)).astype(jnp.bfloat16)
                multiply = functools.partial(jnp.dot, preferred_element_type=jnp.float32)
                out = multiply(upper, BAND[slot, 0]) + (
                    multiply(lower, BAND[slot, 0]) + multiply(upper, BAND[slot, 1])
                )
                TT[v, pl.ds(g * G, G)] = out.reshape(G, R, T) * MET[...][None]
            return 0
        lax.fori_loop(0, comps, step, 0)

    def lam_block(v, at, count):
        block = SEED[v, pl.ds(at, count + 2 * W)]
        total = block[W : W + count]
        for j in range(taps):
            total = total - cf[taps - 1 - j] * block[j : j + count]
        LAM[v, pl.ds(at, count), pl.ds(PAD, R)] = total

    load_seed.wait()

    def lam_inner(v, _):
        def step(c, _):
            lam_block(v, 2 * W + c * W, W)
            return 0
        return lax.fori_loop(0, (X - 2 * W) // W, step, 0)

    lax.fori_loop(0, comps, lam_inner, 0)

    both(fr_up, fr_dn, has_d, has_u, "recv")
    ft_rim.wait_recv()
    azimuthal(0, lambda v, x: FT[v, pl.ds(x, G)])

    def section_at(v, x, lo, hi):
        total = ST[v, x] + TT[v, x]
        for j in range(taps):
            total = total + dr[j] * FR[v, x, pl.ds(PAD - W + j, R)]
        for j in range(lo, hi):
            total = total + dx[j] * FX[v, x + j]
        return total

    def section_edge(v, _):
        for o in range(W):
            low = section_at(v, o, W - o, taps)
            SSEND[0, v, o] = low
            SEC[v, W + o] = low
            x = X - W + o
            high = section_at(v, x, 0, taps - 1 - o)
            SSEND[1, v, o] = high
            SEC[v, W + x] = high
        return 0

    lax.fori_loop(0, comps, section_edge, 0)

    def section_inner(v, _):
        def step(c, _):
            for o in range(2):
                x = W + 2 * c + o
                SEC[v, W + x] = section_at(v, x, 0, taps)
            return 0
        return lax.fori_loop(0, (X - 2 * W) // 2, step, 0)

    lax.fori_loop(0, comps, section_inner, 0)

    both(seed_up, seed_dn, has_l, has_r, "send")
    both(sec_up, sec_dn, has_l, has_r, "start")

    both(seed_up, seed_dn, has_l, has_r, "recv")

    def lam_edges(v, _):
        for at in (0, W, X, X + W):
            lam_block(v, at, W)
        return 0

    lax.fori_loop(0, comps, lam_edges, 0)
    clear(no_l, LAM, (pl.ds(0, W), pl.ds(PAD, R)))
    clear(no_r, LAM, (pl.ds(X + W, W), pl.ds(PAD, R)))
    both(lam_up, lam_dn, has_d, has_u, "start")
    pack(1, lambda v, x: LAM[v, x + W, pl.ds(PAD, R)])
    lam_rim.start()

    both(fx_up, fx_dn, has_l, has_r, "recv")

    def section_rest(v, _):
        for o in range(W):
            low = SEC[v, W + o]
            for j in range(W - o):
                low = low + dx[j] * FX[v, o + j]
            SEC[v, W + o] = low
            x = X - W + o
            high = SEC[v, W + x]
            for j in range(taps - 1 - o, taps):
                high = high + dx[j] * FX[v, x + j]
            SEC[v, W + x] = high
        return 0

    lax.fori_loop(0, comps, section_rest, 0)

    def new_block(v, x, count):
        block = SEC[v, pl.ds(x, count + 2 * W)]
        total = block[W : W + count]
        for j in range(taps):
            total = total - cf[j] * block[j : j + count]
        NEW[v, pl.ds(x, count)] = total

    def new_inner(v, _):
        def step(c, _):
            new_block(v, W + c * W, W)
            return 0
        return lax.fori_loop(0, (X - 2 * W) // W, step, 0)

    lax.fori_loop(0, comps, new_inner, 0)
    inner = pl.ds(W, X - 2 * W)
    store_inner = pltpu.make_async_copy(NEW.at[:, inner], new_out.at[:, inner], local_sem.at[2])
    store_inner.start()

    both(lam_up, lam_dn, has_d, has_u, "recv")
    lam_rim.wait_recv()
    azimuthal(1, lambda v, x: LAM[v, pl.ds(x + W, G), pl.ds(PAD, R)])

    def adjoint_step(x, _):
        q = [ST[v, x] for v in range(comps)]
        grads = [[], [], []]
        for v in range(comps):
            along_x = dx[taps - 1] * LAM[v, x, pl.ds(PAD, R)]
            along_r = dr[taps - 1] * LAM[v, x + W, pl.ds(PAD - W, R)]
            for j in range(1, taps):
                along_x = along_x + dx[taps - 1 - j] * LAM[v, x + j, pl.ds(PAD, R)]
                along_r = along_r + dr[taps - 1 - j] * LAM[v, x + W, pl.ds(PAD - W + j, R)]
            grads[0].append(along_x)
            grads[1].append(along_r)
            grads[2].append(TT[v, x])
        result = pull_back(q, grads)
        for v in range(comps):
            ADJ[v, x] = LAM[v, x + W, pl.ds(PAD, R)] + result[v]
        return 0

    lax.fori_loop(0, X, adjoint_step, 0)
    store_adj = pltpu.make_async_copy(ADJ, adj_out, local_sem.at[3])
    store_adj.start()

    both(sec_up, sec_dn, has_l, has_r, "recv")

    @pl.when(has_l)
    def _():
        def step(v, _):
            for o in range(W):
                total = SEC[v, o]
                for j in range(taps - 1 - o, taps):
                    total = total + dx[j] * FX[v, o + j - W]
                SEC[v, o] = total
            return 0
        lax.fori_loop(0, comps, step, 0)

    @pl.when(has_r)
    def _():
        def step(v, _):
            for o in range(W):
                total = SEC[v, X + W + o]
                for j in range(W - o):
                    total = total + dx[j] * FX[v, X + o + j]
                SEC[v, X + W + o] = total
            return 0
        lax.fori_loop(0, comps, step, 0)

    def new_edges(v, _):
        new_block(v, 0, W)
        new_block(v, X - W, W)
        return 0

    lax.fori_loop(0, comps, new_edges, 0)
    low, high = pl.ds(0, W), pl.ds(X - W, W)
    store_low = pltpu.make_async_copy(NEW.at[:, low], new_out.at[:, low], local_sem.at[4])
    store_high = pltpu.make_async_copy(NEW.at[:, high], new_out.at[:, high], local_sem.at[5])
    store_low.start()
    store_high.start()

    both(fx_up, fx_dn, has_l, has_r, "send")
    both(sec_up, sec_dn, has_l, has_r, "send")
    both(fr_up, fr_dn, has_d, has_u, "send")
    both(lam_up, lam_dn, has_d, has_u, "send")
    ft_rim.wait_send()
    lam_rim.wait_send()
    store_inner.wait()
    store_adj.wait()
    store_low.wait()
    store_high.wait()


def shards(state, adjoint_seed, coef_x, coef_r, coef_t, coef_filter, metric):
    comps, X, R, T = state.shape
    W = (coef_x.shape[0] - 1) // 2
    G = T // (2 * W)
    counts = (lax.axis_size("gx"), lax.axis_size("row"))
    anywhere = pl.BlockSpec(memory_space=pl.ANY)
    scalars = pl.BlockSpec(memory_space=pltpu.SMEM)
    f32 = jnp.float32
    shape = jax.ShapeDtypeStruct(state.shape, f32)
    return pl.pallas_call(
        functools.partial(kernel, counts),
        out_shape=(shape, shape),
        in_specs=[anywhere, anywhere] + [scalars] * 5,
        out_specs=(anywhere, anywhere),
        scratch_shapes=[
            pltpu.VMEM((comps, X, R, T), f32),
            pltpu.VMEM((comps, X + 4 * W, R, T), f32),
            pltpu.VMEM((comps, X + 2 * W, R, T), f32),
            pltpu.VMEM((comps, X, R + 2 * PAD, T), f32),
            pltpu.VMEM((comps, X, R, T), f32),
            pltpu.VMEM((comps, X + 2 * W, R + 2 * PAD, T), f32),
            pltpu.VMEM((comps, X + 2 * W, R, T), f32),
            pltpu.VMEM((2, comps, W, R, T), f32),
            pltpu.VMEM((comps, X, R, T), f32),
            pltpu.VMEM((comps, X, R, T), f32),
            pltpu.VMEM((comps, X, R, T), f32),
            pltpu.VMEM((2, 2, 2 * T, T), jnp.bfloat16),
            pltpu.VMEM((R, T), f32),
            pltpu.VMEM((2, comps, X // G, R, T), f32),
            pltpu.VMEM((2, comps, X // G, R, T), f32),
            pltpu.SemaphoreType.DMA((6,)),
            pltpu.SemaphoreType.DMA((12,)),
            pltpu.SemaphoreType.DMA((12,)),
        ],
        compiler_params=pltpu.CompilerParams(
            collective_id=0, has_side_effects=True, vmem_limit_bytes=60 * 2**20
        ),
    )(state, adjoint_seed, coef_x, coef_r, coef_t, coef_filter, metric)


def solution(mesh):
    placed = (P(None, "gx", "row", "th"), P(None, "gx", "row", "th"), P(), P(), P(), P(), P("row"))
    return jax.shard_map(
        shards,
        mesh=mesh,
        in_specs=placed,
        out_specs=(P(None, "gx", "row", "th"), P(None, "gx", "row", "th")),
        check_vma=False,
    )
```
